256 devices in a mesh: ctx: 64 (over y, z, core), head: 4 (over x).
Axes of the slice: x: 4, y: 4, z: 8, core: 2. Of those that a mesh axis runs over, the one named last changes fastest.
Arguments:
- queries: bfloat16 [16384, 2048], P('ctx', 'head'), may hold values from -6 to 6
- keys: bfloat16 [16384, 2048], P('ctx', 'head'), may hold values from -6 to 6
- values: bfloat16 [16384, 2048], P('ctx', 'head'), may hold values from -6 to 6
- out_grad: bfloat16 [16384, 2048], P('ctx', 'head'), may hold values from -6 to 6
- doc_lengths: int32 [32], replicated, may hold values from 1 to 768, as said below
Outputs:
- attended: float32 [16384, 2048], P('ctx', 'head')
- query_grad: float32 [16384, 2048], P('ctx', 'head')
- key_grad: float32 [16384, 2048], P('ctx', 'head')
- value_grad: float32 [16384, 2048], P('ctx', 'head')
The draws below stay inside these ranges and needn't reach their ends.
Inputs may be any that keep to these rules, and one draw needn't show every extreme that they name: `doc_lengths`: the first document has exactly 768 tokens, every other one 1 to 768, and all lengths sum to 16384.
All inputs are finite; a program needn't handle non-finite values.
Results may differ from the reference program's by a relative error of at most 0.0095.
Values may be sent and summed in bfloat16 or wider, within the bound.
No kernel may reach another device: no remote copies, remote signals or barrier semaphores. Data moves between devices by JAX's collectives and lax.ppermute only.
A program may use at most 64 MiB of HBM per device.

```python
import jax
import jax.numpy as jnp
from jax import lax

HEADS = 16
HD = 128
TOK_DEV = 256
TOKENS = 16384
PROMPT = 64
SPAN = 3
DOC_MOST = 768
DOCS = 32
N_CTX = 64


def draw_queries(key, part):
    key = jax.random.fold_in(key, 1)
    drawn = jnp.clip(jax.random.normal(key, (TOKENS, HEADS * HD), jnp.float32), -6.0, 6.0)
    return drawn.astype(jnp.bfloat16)


def draw_keys(key, part):
    key = jax.random.fold_in(key, 2)
    drawn = jnp.clip(jax.random.normal(key, (TOKENS, HEADS * HD), jnp.float32), -6.0, 6.0)
    return drawn.astype(jnp.bfloat16)


def draw_doc_lengths(key, part):
    key = jax.random.fold_in(key, 3)
    remaining = TOKENS - DOC_MOST
    others = DOCS - 1
    places = jnp.arange(others, dtype=jnp.int32)
    even_split = (places + 1) * remaining // others - places * remaining // others
    least = remaining // others
    spread = max(0, min(least - 1, DOC_MOST - least - 1) // 2)
    moves = jax.random.randint(key, (others,), -spread, spread + 1)
    lengths = even_split + moves - jnp.roll(moves, -1)
    return jnp.concatenate([jnp.full((1,), DOC_MOST, jnp.int32), lengths.astype(jnp.int32)])


def steps_of(stream_key, shape, shards, low, top_value):
    def one(axis_at, blocks):
        heights = jax.random.uniform(jax.random.fold_in(jax.random.fold_in(stream_key, 6), axis_at), (blocks,), jnp.float32, low / len(shards), top_value / len(shards))
        return jnp.repeat(jnp.exp(heights), shape[axis_at] // blocks).reshape((-1,) + (1,) * (len(shape) - axis_at - 1))

    level = one(*shards[0])
    for cut in shards[1:]:
        level = level * one(*cut)
    return level


def scatter_about(key, dims, width, most, shards=(), kind=jnp.bfloat16):
    values = jax.random.normal(key, dims, jnp.float32) * width
    if len(shards) > 0:
        values = steps_of(key, dims, shards, -0.22, 0.18) * values
    return jnp.clip(values, min=-most, max=most).astype(kind)


def setup_inputs(seed: int = 0) -> dict:
    key_of = jax.random.split(jax.random.key(seed), 6)
    queries = draw_queries(jax.random.fold_in(key_of[5], 71), 0)
    keys = draw_keys(jax.random.fold_in(key_of[5], 71), 0)
    values = scatter_about(key_of[2], (TOKENS, HEADS * HD), 1.0, 6.0, ((0, 64), (1, 4)))
    out_grad = scatter_about(key_of[3], (TOKENS, HEADS * HD), 1.0, 6.0, ((0, 64), (1, 4)))
    doc_lengths = draw_doc_lengths(jax.random.fold_in(key_of[5], 71), 0)
    return dict(queries=queries, keys=keys, values=values, out_grad=out_grad, doc_lengths=doc_lengths)


def segment_ids(doc_lengths, positions):
    doc_ends = jnp.cumsum(doc_lengths).astype(jnp.int32)
    return jnp.sum((doc_ends[None, :] <= positions[:, None]).astype(jnp.int32), axis=1).astype(jnp.int32)


def reference(queries, keys, values, out_grad, doc_lengths):
    score_scale = 1.0 / (HD ** 0.5)
    window = (SPAN + 1) * TOK_DEV
    front = SPAN * TOK_DEV
    q_all = queries.reshape(TOKENS, HEADS, HD)
    k_all = keys.reshape(TOKENS, HEADS, HD)
    v_all = values.reshape(TOKENS, HEADS, HD)
    dout_all = out_grad.reshape(TOKENS, HEADS, HD)
    k_prompt = k_all[:PROMPT]
    v_prompt = v_all[:PROMPT]
    prompt_pos = jnp.arange(PROMPT, dtype=jnp.int32)
    k_pad = jnp.concatenate([jnp.zeros((front, HEADS, HD), keys.dtype), k_all], axis=0)
    v_pad = jnp.concatenate([jnp.zeros((front, HEADS, HD), values.dtype), v_all], axis=0)
    seg_all = segment_ids(doc_lengths, jnp.arange(TOKENS, dtype=jnp.int32))
    seg_pad = jnp.concatenate([-jnp.ones((front,), jnp.int32), seg_all]).astype(jnp.int32)

    def tile_setup(index):
        start = (index * TOK_DEV).astype(jnp.int32)
        q_blk = lax.dynamic_slice_in_dim(q_all, start, TOK_DEV, 0)
        k_win = lax.dynamic_slice_in_dim(k_pad, start, window, 0)
        v_win = lax.dynamic_slice_in_dim(v_pad, start, window, 0)
        q_pos = start + jnp.arange(TOK_DEV, dtype=jnp.int32)
        k_pos = start - front + jnp.arange(window, dtype=jnp.int32)
        seg_q = lax.dynamic_slice_in_dim(seg_all, start, TOK_DEV, 0)
        seg_k = lax.dynamic_slice_in_dim(seg_pad, start, window, 0)
        win_ok = (k_pos[None, :] <= q_pos[:, None]) & (seg_q[:, None] == seg_k[None, :]) & (k_pos[None, :] >= PROMPT)
        prompt_ok = prompt_pos[None, :] <= q_pos[:, None]
        allowed = jnp.concatenate([prompt_ok, win_ok], axis=1)
        k_cat = jnp.concatenate([k_prompt, k_win], axis=0)
        v_cat = jnp.concatenate([v_prompt, v_win], axis=0)
        scores = jnp.einsum("thd,uhd->htu", q_blk.astype(jnp.float32), k_cat.astype(jnp.float32)) * score_scale
        return start, q_blk, k_cat, v_cat, allowed, scores

    def forward_block(index):
        start, q_blk, k_cat, v_cat, allowed, scores = tile_setup(index)
        masked = jnp.where(allowed[None], scores, -jnp.inf)
        row_top = jnp.max(masked, axis=2)
        totals = jnp.sum(jnp.exp(masked - row_top[:, :, None]), axis=2)
        lse = row_top + jnp.log(totals)
        probs = jnp.exp(masked - lse[:, :, None])
        out_blk = jnp.einsum("htu,uhd->thd", probs, v_cat.astype(jnp.float32), precision=lax.Precision.HIGHEST)
        return out_blk, lse

    outs, lses = lax.map(forward_block, jnp.arange(N_CTX, dtype=jnp.int32))
    attended = outs.reshape(TOKENS, HEADS * HD)

    def backward_block(carried, index):
        dk_pad, dv_pad, dk_prompt, dv_prompt = carried
        start, q_blk, k_cat, v_cat, allowed, scores = tile_setup(index)
        lse = lses[index]
        out_blk = outs[index]
        dout_blk = lax.dynamic_slice_in_dim(dout_all, start, TOK_DEV, 0)
        delta = jnp.sum(dout_blk.astype(jnp.float32) * out_blk, axis=2).T
        weights = jnp.where(allowed[None], jnp.exp(scores - lse[:, :, None]), 0.0)
        rounded = lax.optimization_barrier(weights.astype(jnp.bfloat16))
        dv_part = jnp.einsum("htu,thd->uhd", rounded.astype(jnp.float32), dout_blk.astype(jnp.float32))
        dprob = jnp.einsum("thd,uhd->htu", dout_blk.astype(jnp.float32), v_cat.astype(jnp.float32))
        dscore = lax.optimization_barrier((weights * (dprob - delta[:, :, None])).astype(jnp.bfloat16))
        dq_blk = jnp.einsum("htu,uhd->thd", dscore.astype(jnp.float32), k_cat.astype(jnp.float32)) * score_scale
        dk_part = jnp.einsum("htu,thd->uhd", dscore.astype(jnp.float32), q_blk.astype(jnp.float32))
        dk_prompt = dk_prompt + dk_part[:PROMPT]
        dv_prompt = dv_prompt + dv_part[:PROMPT]
        dk_pad = lax.dynamic_update_slice_in_dim(dk_pad, lax.dynamic_slice_in_dim(dk_pad, start, window, 0) + dk_part[PROMPT:], start, 0)
        dv_pad = lax.dynamic_update_slice_in_dim(dv_pad, lax.dynamic_slice_in_dim(dv_pad, start, window, 0) + dv_part[PROMPT:], start, 0)
        return (dk_pad, dv_pad, dk_prompt, dv_prompt), dq_blk

    zero_pad = jnp.zeros((front + TOKENS, HEADS, HD), jnp.float32)
    zero_prompt = jnp.zeros((PROMPT, HEADS, HD), jnp.float32)
    (dk_pad, dv_pad, dk_prompt, dv_prompt), dq_blocks = lax.scan(backward_block, (zero_pad, zero_pad, zero_prompt, zero_prompt), jnp.arange(N_CTX, dtype=jnp.int32))
    dk_full = dk_pad[front:]
    dv_full = dv_pad[front:]
    dk_full = jnp.concatenate([dk_full[:PROMPT] + dk_prompt, dk_full[PROMPT:]], axis=0)
    dv_full = jnp.concatenate([dv_full[:PROMPT] + dv_prompt, dv_full[PROMPT:]], axis=0)
    query_grad = dq_blocks.reshape(TOKENS, HEADS * HD)
    key_grad = (dk_full * score_scale).reshape(TOKENS, HEADS * HD)
    value_grad = dv_full.reshape(TOKENS, HEADS * HD)
    return attended, query_grad, key_grad, value_grad
```

```python
import math

import jax
import jax.numpy as jnp
from jax import lax
from jax.experimental import pallas as pl
from jax.experimental.pallas import tpu as pltpu
from jax.sharding import PartitionSpec as P

HD = 128
PROMPT = 64
TOK = 256
NCTX = 64
HEADS = 4
SCALE = 1.0 / math.sqrt(HD)
SCALE2 = SCALE * math.log2(math.e)
NEG = -1e30
FAR = 1 << 28
F32 = jnp.float32
BF16 = jnp.bfloat16
VMEM_LIMIT = 40 * 1024 * 1024


def mm_nt(a, b):
    return lax.dot_general(a, b, (((1,), (1,)), ((), ())), preferred_element_type=F32)


def mm_nn(a, b):
    return lax.dot_general(a, b, (((1,), (0,)), ((), ())), preferred_element_type=F32)


def head_cols(h):
    return pl.ds(h * HD, HD)


def column_of(row):
    return jnp.transpose(jnp.broadcast_to(row, (128, TOK)))[:, :1]


def key_tile(base, width):
    return base + lax.broadcasted_iota(jnp.int32, (1, width), 1)


def query_mask(own, lo_col, q_col, d):
    k_row = key_tile((own - d) * TOK, TOK)
    ok = k_row >= lo_col
    if d == 0:
        ok = ok & (k_row <= q_col)
    return ok


def pick(first, a, b):
    return jnp.where(first, a, b)


def forward_kernel(info, lo_ref, q, do, k0, v0, kv1a, kv1b, kv2, kv3, kvp, att, cols, rows, pgrad):
    own = info[0]
    core0 = info[1] == 0
    lo_col = column_of(lo_ref[0:1, :].astype(F32)).astype(jnp.int32)
    q_col = own * TOK + lax.broadcasted_iota(jnp.int32, (TOK, 1), 0)
    masks = [query_mask(own, lo_col, q_col, d) for d in range(4)]
    masks.append(key_tile(0, PROMPT) <= q_col)
    lane = lax.broadcasted_iota(jnp.int32, (TOK, 128), 1)
    packed = jnp.zeros((TOK, 128), F32)
    for h in range(HEADS):
        c = head_cols(h)
        qh = q[:, c]
        doh = do[:, c]
        keys = [
            k0[:, c],
            pick(core0, kv1a[:TOK, c], kv1b[:TOK, c]),
            kv2[:TOK, c],
            kv3[:TOK, c],
            kvp[:PROMPT, c],
        ]
        vals = [
            v0[:, c],
            pick(core0, kv1a[TOK:, c], kv1b[TOK:, c]),
            kv2[TOK:, c],
            kv3[TOK:, c],
            kvp[PROMPT:, c],
        ]
        scores = [jnp.where(ok, mm_nt(qh, kk) * SCALE2, NEG) for ok, kk in zip(masks, keys)]
        top = jnp.max(scores[4], axis=1, keepdims=True)
        for s in scores[:4]:
            top = jnp.maximum(top, jnp.max(s, axis=1, keepdims=True))
        total = jnp.zeros((TOK, 1), F32)
        acc = jnp.zeros((TOK, HD), F32)
        for s, vv in zip(scores, vals):
            p = jnp.exp2(s - top)
            total = total + jnp.sum(p, axis=1, keepdims=True)
            acc = acc + mm_nn(p.astype(BF16), vv)
        out = acc / total
        att[:, c] = out
        delta = jnp.sum(out * doh.astype(F32), axis=1, keepdims=True)
        packed = jnp.where(lane == h, top + jnp.log2(total), packed)
        packed = jnp.where(lane == HEADS + h, delta, packed)
    cols[...] = packed
    turned = jnp.transpose(packed)[:8, :]
    rows[...] = turned
    u_col = lax.broadcasted_iota(jnp.int32, (PROMPT, 1), 0)
    q_row = key_tile(own * TOK, TOK)
    ok = u_col <= q_row
    for h in range(HEADS):
        c = head_cols(h)
        dk, dv = key_side(
            kvp[:PROMPT, c], kvp[PROMPT:, c], q[:, c], do[:, c], turned[h : h + 1], turned[HEADS + h : HEADS + h + 1], ok
        )
        pgrad[:PROMPT, c] = (dk * SCALE).astype(BF16)
        pgrad[PROMPT:, c] = dv.astype(BF16)


def key_side(kk, vv, qq, dd, lse_row, delta_row, ok):
    s = mm_nt(kk, qq) * SCALE2
    p = jnp.where(ok, jnp.exp2(s - lse_row), 0.0)
    dv = mm_nn(p.astype(BF16), dd)
    ds = (p * (mm_nt(vv, dd) - delta_row)).astype(BF16)
    return mm_nn(ds, qq), dv


def query_grad_kernel(info, lo_ref, cols, q, do, k0, v0, kv1a, kv1b, kv2, kv3, kvp, dq):
    own = info[0]
    core0 = info[1] == 0
    lo_col = column_of(lo_ref[0:1, :].astype(F32)).astype(jnp.int32)
    q_col = own * TOK + lax.broadcasted_iota(jnp.int32, (TOK, 1), 0)
    masks = [query_mask(own, lo_col, q_col, d) for d in range(4)]
    masks.append(key_tile(0, PROMPT) <= q_col)
    for h in range(HEADS):
        c = head_cols(h)
        qh = q[:, c]
        doh = do[:, c]
        keys = [
            k0[:, c],
            pick(core0, kv1a[:TOK, c], kv1b[:TOK, c]),
            kv2[:TOK, c],
            kv3[:TOK, c],
            kvp[:PROMPT, c],
        ]
        vals = [
            v0[:, c],
            pick(core0, kv1a[TOK:, c], kv1b[TOK:, c]),
            kv2[TOK:, c],
            kv3[TOK:, c],
            kvp[PROMPT:, c],
        ]
        lse = cols[:, h : h + 1]
        delta = cols[:, HEADS + h : HEADS + h + 1]
        acc = jnp.zeros((TOK, HD), F32)
        for ok, kk, vv in zip(masks, keys, vals):
            p = jnp.where(ok, jnp.exp2(mm_nt(qh, kk) * SCALE2 - lse), 0.0)
            ds = (p * (mm_nt(doh, vv) - delta)).astype(BF16)
            acc = acc + mm_nn(ds, kk)
        dq[:, c] = acc * SCALE


def key_grad_kernel(info, lo_ref, r0, r1, r2, r3, k, v, q0, do0, qd1a, qd1b, qd2, qd3, dk, dv):
    own = info[0]
    core0 = info[1] == 0
    k_col = own * TOK + lax.broadcasted_iota(jnp.int32, (TOK, 1), 0)
    masks = []
    for d in range(4):
        ok = k_col >= lo_ref[d : d + 1, :]
        if d == 0:
            ok = ok & (k_col <= key_tile(own * TOK, TOK))
        masks.append(ok)
    for h in range(HEADS):
        c = head_cols(h)
        qs = [q0[:, c], pick(core0, qd1a[:TOK, c], qd1b[:TOK, c]), qd2[:TOK, c], qd3[:TOK, c]]
        ds = [do0[:, c], pick(core0, qd1a[TOK:, c], qd1b[TOK:, c]), qd2[TOK:, c], qd3[TOK:, c]]
        dk_acc = jnp.zeros((TOK, HD), F32)
        dv_acc = jnp.zeros((TOK, HD), F32)
        for d, r in enumerate((r0, r1, r2, r3)):
            a, b = key_side(
                k[:, c], v[:, c], qs[d], ds[d], r[h : h + 1, :], r[HEADS + h : HEADS + h + 1, :], masks[d]
            )
            dk_acc = dk_acc + a
            dv_acc = dv_acc + b
        dk[:, c] = dk_acc * SCALE
        dv[:, c] = dv_acc


def finish_kernel(info, dk_in, dv_in, pk, pv, dk, dv):
    first = info[0] == 0
    dk[...] = dk_in[...] + jnp.where(first, pk[...], 0.0)
    dv[...] = dv_in[...] + jnp.where(first, pv[...], 0.0)


def call(kernel, outs, scalars, flops, *args):
    smem = pl.BlockSpec(memory_space=pltpu.SMEM)
    vmem = pl.BlockSpec(memory_space=pltpu.VMEM)
    return pl.pallas_call(
        kernel,
        out_shape=[jax.ShapeDtypeStruct(s, t) for s, t in outs],
        in_specs=[smem] * scalars + [vmem] * (len(args) - scalars),
        out_specs=[vmem] * len(outs),
        compiler_params=pltpu.CompilerParams(vmem_limit_bytes=VMEM_LIMIT),
        cost_estimate=pl.CostEstimate(flops=flops, bytes_accessed=4 << 20, transcendentals=1 << 20),
    )(*args)


def shift(x, by):
    return lax.ppermute(x, "ctx", [(i, (i + by) % NCTX) for i in range(NCTX)])


def swap(x):
    return lax.ppermute(x, "ctx", [(i, i ^ 1) for i in range(NCTX)])


def at(y, z, c):
    return (y * 8 + z) * 2 + c


Z_ORDER = (4, 5, 3, 6, 2, 7, 1)


def spread_prompt(mine, own):
    held = jnp.where(own == 0, mine, 0).astype(BF16)
    got = [lax.ppermute(held, "ctx", [(0, at(0, z, 0))]) for z in Z_ORDER]
    held = sum(got, held)
    got = [
        lax.ppermute(held, "ctx", [(at(0, z, 0), at(y, z, 0)) for z in range(8)]) for y in (2, 3, 1)
    ]
    held = sum(got, held)
    return jnp.where(own % 2 == 0, held, swap(held))


def gather_prompt(pgrad, own):
    core0 = own % 2 == 0
    dk, dv = pgrad[:PROMPT], pgrad[PROMPT:]
    other = swap(jnp.where(core0, dv, dk))
    part = jnp.where(core0, dk, dv).astype(F32) + other.astype(F32)
    sent = part.astype(BF16)
    got = [
        lax.ppermute(sent, "ctx", [(at(y, z, c), at(y, 0, c)) for y in range(4) for c in range(2)])
        for z in Z_ORDER
    ]
    part = sum([g.astype(F32) for g in got], part)
    sent = part.astype(BF16)
    got = [lax.ppermute(sent, "ctx", [(at(y, 0, c), at(0, 0, c)) for c in range(2)]) for y in (2, 3, 1)]
    part = sum([g.astype(F32) for g in got], part)
    other = swap(part.astype(BF16)).astype(F32)
    return part, other


def on_device(q, k, v, do, doc_lengths):
    own = lax.axis_index("ctx")
    core0 = own % 2 == 0
    info = jnp.stack([own, own % 2]).astype(jnp.int32)
    ends = jnp.cumsum(doc_lengths).astype(jnp.int32)
    blocks = own + jnp.arange(8, dtype=jnp.int32)
    pos = blocks[:, None] * TOK + jnp.arange(TOK, dtype=jnp.int32)[None, :]
    starts = jnp.max(jnp.where(ends[:, None, None] <= pos[None], ends[:, None, None], 0), axis=0)
    lo = jnp.where(blocks[:, None] < NCTX, jnp.maximum(starts, PROMPT), FAR)

    kv = jnp.concatenate([k, v], axis=0)
    qd = jnp.concatenate([q, do], axis=0)
    kv2 = shift(kv, 2)
    qd2 = shift(qd, -2)
    first = swap(jnp.where(core0, kv, qd))
    kvp = spread_prompt(jnp.concatenate([k[:PROMPT], v[:PROMPT]], axis=0), own)
    second = swap(jnp.where(core0, qd2, kv2))
    kv3 = shift(kv2, 1)
    qd3 = shift(qd2, -1)

    tok = (TOK, HEADS * HD)
    att, cols, rows, pgrad = call(
        forward_kernel,
        [(tok, F32), ((TOK, 128), F32), ((8, TOK), F32), ((2 * PROMPT, HEADS * HD), BF16)],
        1,
        600_000_000,
        info, lo, q, do, k, v, second, first, kv2, kv3, kvp,
    )
    r1, r2, r3 = shift(rows, -1), shift(rows, -2), shift(rows, -3)
    part, other = gather_prompt(pgrad, own)
    (dq,) = call(
        query_grad_kernel, [(tok, F32)], 1, 850_000_000,
        info, lo, cols, q, do, k, v, second, first, kv2, kv3, kvp,
    )
    dk, dv = call(
        key_grad_kernel, [(tok, F32), (tok, F32)], 1, 1_100_000_000,
        info, lo, rows, r1, r2, r3, k, v, q, do, first, second, qd2, qd3,
    )
    head_block = pl.BlockSpec((PROMPT, HEADS * HD), lambda i: (0, 0))
    dk, dv = pl.pallas_call(
        finish_kernel,
        grid=(1,),
        out_shape=[jax.ShapeDtypeStruct(tok, F32)] * 2,
        in_specs=[pl.BlockSpec(memory_space=pltpu.SMEM)] + [head_block] * 4,
        out_specs=[head_block] * 2,
        input_output_aliases={1: 0, 2: 1},
    )(info, dk, dv, part, other)
    return att, dq, dk, dv


def solution(mesh):
    spec = P("ctx", "head")
    return jax.shard_map(
        on_device, mesh=mesh, in_specs=(spec,) * 4 + (P(),), out_specs=(spec,) * 4, check_vma=False
    )
```

```python
import math

import jax
import jax.numpy as jnp
from jax import lax
from jax.experimental import pallas as pl
from jax.experimental.pallas import tpu as pltpu
from jax.sharding import PartitionSpec as P

HD = 128
PROMPT = 64
TOK = 256
NCTX = 64
HEADS = 4
WIDE = HEADS * HD
SCALE = 1.0 / math.sqrt(HD)
SCALE2 = SCALE * math.log2(math.e)
NEG = -1e30
FAR = 1 << 28
F32 = jnp.float32
BF16 = jnp.bfloat16
VMEM_LIMIT = 40 * 1024 * 1024
GATE_R = False
GATE_DQ = True
GATE_Y = True
GATE_DK = True
SPREAD_GATE = True
HALO_DONE = True
Y_FILL = True
Z_FILL = True
Y_STEPS_FILL = False


def mm_nt(a, b):
    return lax.dot_general(a, b, (((1,), (1,)), ((), ())), preferred_element_type=F32)


def mm_nn(a, b):
    return lax.dot_general(a, b, (((1,), (0,)), ((), ())), preferred_element_type=F32)


def mm_tn(a, b):
    return lax.dot_general(a, b, (((0,), (0,)), ((), ())), preferred_element_type=F32)


def head(h):
    return pl.ds(h * HD, HD)


def key_index(base, count):
    return base + lax.broadcasted_iota(jnp.int32, (count, TOK), 0)


def query_index(own):
    return own * TOK + lax.broadcasted_iota(jnp.int32, (1, TOK), 1)


def fold(state, qh, tiles):
    top, total, acc = state
    scores = [jnp.where(ok, mm_nt(kk, qh) * SCALE2, NEG) for ok, kk, _ in tiles]
    new_top = top
    for s in scores:
        new_top = jnp.maximum(new_top, jnp.max(s, axis=0, keepdims=True))
    fade = jnp.exp2(top - new_top)
    total = total * fade
    acc = acc * fade
    for s, (_, _, vv) in zip(scores, tiles):
        p = jnp.exp2(s - new_top)
        total = total + jnp.sum(p, axis=0, keepdims=True)
        acc = acc + mm_tn(vv, p.astype(BF16))
    return (new_top, total, acc), scores


def load_state(stat, acc, h):
    return stat[h : h + 1, :], stat[HEADS + h : HEADS + h + 1, :], acc[head(h), :]


def store_state(stat, acc, h, state):
    stat[h : h + 1, :], stat[HEADS + h : HEADS + h + 1, :], acc[head(h), :] = state


def pack_kernel(info, k, v, q, do, kv, qd, sel, kvp, sems):
    top, bottom = pl.ds(0, TOK), pl.ds(TOK, TOK)
    jobs = [(k, kv.at[top]), (v, kv.at[bottom]), (q, qd.at[top]), (do, qd.at[bottom])]
    copies = [pltpu.make_async_copy(a, b, sems.at[i]) for i, (a, b) in enumerate(jobs)]
    for copy in copies:
        copy.start()
    copies[0].wait()
    copies[1].wait()
    kvp[:PROMPT, :] = kv[:PROMPT, :]
    kvp[PROMPT:, :] = kv[pl.ds(TOK, PROMPT), :]
    copies[2].wait()
    copies[3].wait()
    sel[...] = jnp.where(info[1] == 0, kv[...], qd[...])


def own_kernel(info, lo_ref, q, k, v, do, stat, acc, do_t):
    own = info[0]
    k_pos = key_index(own * TOK, TOK)
    ok = (k_pos >= lo_ref[0:1, :]) & (k_pos <= query_index(own))
    for h in range(HEADS):
        c = head(h)
        start = (jnp.full((1, TOK), NEG, F32), jnp.zeros((1, TOK), F32), jnp.zeros((HD, TOK), F32))
        state, _ = fold(start, q[:, c], [(ok, k[:, c], v[:, c])])
        store_state(stat, acc, h, state)
        do_t[c, :] = jnp.transpose(do[:, c].astype(F32))


def near_kernel(info, lo_ref, stat_in, acc_in, q, kv1a, kv1b, kv2, stat, acc):
    own = info[0]
    core0 = info[1] == 0
    ok1 = key_index((own - 1) * TOK, TOK) >= lo_ref[0:1, :]
    ok2 = key_index((own - 2) * TOK, TOK) >= lo_ref[0:1, :]
    for h in range(HEADS):
        c = head(h)
        kk = jnp.where(core0, kv1a[:TOK, c], kv1b[:TOK, c])
        vv = jnp.where(core0, kv1a[TOK:, c], kv1b[TOK:, c])
        tiles = [(ok1, kk, vv), (ok2, kv2[:TOK, c], kv2[TOK:, c])]
        state, _ = fold(load_state(stat_in, acc_in, h), q[:, c], tiles)
        store_state(stat, acc, h, state)


def last_kernel(info, lo_ref, stat, acc, q, do, do_t, kv3, kvp, out_t, rows, pk, pv):
    own = info[0]
    ok3 = key_index((own - 3) * TOK, TOK) >= lo_ref[0:1, :]
    okp = key_index(0, PROMPT) <= query_index(own)
    dprobs = [mm_nt(kvp[PROMPT:, head(h)], do[:, head(h)]) for h in range(HEADS)]
    folded = []
    for h in range(HEADS):
        c = head(h)
        tiles = [(ok3, kv3[:TOK, c], kv3[TOK:, c]), (okp, kvp[:PROMPT, c], kvp[PROMPT:, c])]
        folded.append(fold(load_state(stat, acc, h), q[:, c], tiles))
    for h in range(HEADS):
        c = head(h)
        (top, total, done), scores = folded[h]
        out = done * (1.0 / total)
        lse = top + jnp.log2(total)
        delta = jnp.sum(out * do_t[c, :], axis=0, keepdims=True)
        out_t[c, :] = out
        rows[h : h + 1, :] = lse
        rows[HEADS + h : HEADS + h + 1, :] = delta
        p = jnp.exp2(scores[1] - lse)
        ds = (p * (dprobs[h] - delta)).astype(BF16)
        pv[:, c] = mm_nn(p.astype(BF16), do[:, c]).astype(BF16)
        pk[:, c] = (mm_nn(ds, q[:, c]) * SCALE).astype(BF16)


def grads(ok, kk, vv, qh, doh, lse, delta):
    p = jnp.where(ok, jnp.exp2(mm_nt(kk, qh) * SCALE2 - lse), 0.0)
    ds = p * (mm_nt(vv, doh) - delta)
    return p.astype(BF16), ds.astype(BF16)


def query_grad_kernel(
    info, lo_ref, rows, out_t, q, do, k, v, kv1a, kv1b, kv2, kv3, kvp, att, dq, dk, dv
):
    own = info[0]
    core0 = info[1] == 0
    k_pos = key_index(own * TOK, TOK)
    low = lo_ref[0:1, :]
    masks = [(k_pos >= low) & (k_pos <= query_index(own))]
    masks += [key_index((own - d) * TOK, TOK) >= low for d in (1, 2, 3)]
    masks.append(key_index(0, PROMPT) <= query_index(own))
    for h in range(HEADS):
        c = head(h)
        qh, doh = q[:, c], do[:, c]
        lse, delta = rows[h : h + 1, :], rows[HEADS + h : HEADS + h + 1, :]
        keys = [k[:, c], jnp.where(core0, kv1a[:TOK, c], kv1b[:TOK, c]), kv2[:TOK, c], kv3[:TOK, c]]
        vals = [v[:, c], jnp.where(core0, kv1a[TOK:, c], kv1b[TOK:, c]), kv2[TOK:, c], kv3[TOK:, c]]
        keys.append(kvp[:PROMPT, c])
        vals.append(kvp[PROMPT:, c])
        total = jnp.zeros((HD, TOK), F32)
        for i, (ok, kk, vv) in enumerate(zip(masks, keys, vals)):
            p, ds = grads(ok, kk, vv, qh, doh, lse, delta)
            total = total + mm_tn(kk, ds)
            if i == 0:
                dk[:, c] = mm_nn(ds, qh)
                dv[:, c] = mm_nn(p, doh)
        dq[:, c] = jnp.transpose(total * SCALE)
        att[:, c] = jnp.transpose(out_t[c, :])


def key_grad_kernel(
    info, lo_ref, r1, r2, r3, dk_own, dv_own, k, v, qd1a, qd1b, qd2, qd3, dk, dv, dk_top, dv_top
):
    own = info[0]
    core0 = info[1] == 0
    k_pos = key_index(own * TOK, TOK)
    masks = [k_pos >= lo_ref[d : d + 1, :] for d in (1, 2, 3)]
    for h in range(HEADS):
        c = head(h)
        kk, vv = k[:, c], v[:, c]
        qs = [jnp.where(core0, qd1a[:TOK, c], qd1b[:TOK, c]), qd2[:TOK, c], qd3[:TOK, c]]
        dos = [jnp.where(core0, qd1a[TOK:, c], qd1b[TOK:, c]), qd2[TOK:, c], qd3[TOK:, c]]
        dk_sum, dv_sum = dk_own[:, c], dv_own[:, c]
        for ok, qq, dd, r in zip(masks, qs, dos, (r1, r2, r3)):
            lse, delta = r[h : h + 1, :], r[HEADS + h : HEADS + h + 1, :]
            p, ds = grads(ok, kk, vv, qq, dd, lse, delta)
            dk_sum = dk_sum + mm_nn(ds, qq)
            dv_sum = dv_sum + mm_nn(p, dd)
        dk_sum = dk_sum * SCALE
        dk[:, c] = dk_sum
        dv[:, c] = dv_sum
        dk_top[:, c] = dk_sum[:PROMPT]
        dv_top[:, c] = dv_sum[:PROMPT]


def finish_kernel(info, part, other, dk_top, dv_top, dk_in, dv_in, dk, dv, dk_buf, dv_buf, sems):
    first = info[0] == 0
    dk_buf[...] = dk_top[...] + jnp.where(first, part[...], 0.0)
    dv_buf[...] = dv_top[...] + jnp.where(first, other[...].astype(F32), 0.0)
    rows = pl.ds(0, PROMPT)
    copies = [
        pltpu.make_async_copy(dk_buf, dk.at[rows], sems.at[0]),
        pltpu.make_async_copy(dv_buf, dv.at[rows], sems.at[1]),
    ]
    for copy in copies:
        copy.start()
    for copy in copies:
        copy.wait()


def call(kernel, outs, scalars, flops, *args):
    smem = pl.BlockSpec(memory_space=pltpu.SMEM)
    vmem = pl.BlockSpec(memory_space=pltpu.VMEM)
    return pl.pallas_call(
        kernel,
        out_shape=[jax.ShapeDtypeStruct(s, t) for s, t in outs],
        in_specs=[smem] * scalars + [vmem] * (len(args) - scalars),
        out_specs=[vmem] * len(outs),
        compiler_params=pltpu.CompilerParams(vmem_limit_bytes=VMEM_LIMIT),
        cost_estimate=pl.CostEstimate(flops=flops, bytes_accessed=4 << 20, transcendentals=1 << 20),
    )(*args)


def shift(x, by):
    return lax.ppermute(x, "ctx", [(i, (i + by) % NCTX) for i in range(NCTX)])


def swap(x):
    return lax.ppermute(x, "ctx", [(i, i ^ 1) for i in range(NCTX)])


def at(y, z, c):
    return (y * 8 + z) * 2 + c


def deliver(x, pairs):
    return lax.ppermute(x, "ctx", pairs)


def exchange(x, pairs):
    to = {i: i ^ 1 for i in range(NCTX)}
    for a, b in pairs:
        to[a], to[b] = b, a
    return lax.ppermute(x, "ctx", sorted(to.items()))


Z_ORDER = (4, 5, 3, 6, 2, 7, 1)
Y_ORDER = (2, 3, 1)
SPREAD = (
    ([(at(0, 0, 0), at(0, 4, 0))],),
    tuple([(at(0, n, 0), at(0, n + k, 0)) for n in (0, 4)] for k in (3, 2, 1)),
    tuple([(at(0, n, 0), at(k, n, 0)) for n in range(8)] for k in Y_ORDER),
)


def spread(held, own, steps):
    for step in steps:
        got = [deliver(held, pairs) for pairs in step]
        for pairs, g in zip(step, got):
            takes = sum([own == b for _, b in pairs], jnp.int32(0)) > 0
            held = jnp.where(takes, g, held)
    return held


def gather_cores(pk, pv, c):
    other = swap(jnp.where(c == 0, pv, pk))
    return jnp.where(c == 0, pk, pv).astype(F32) + other.astype(F32)


def gather_z(part):
    route = exchange if Z_FILL else deliver
    return [
        route(part, [(at(m, n, i), at(m, 0, i)) for m in range(4) for i in range(2)]) for n in Z_ORDER
    ]


def gather_y(part):
    route = exchange if Y_FILL else deliver
    return [route(part, [(at(m, 0, i), at(0, 0, i)) for i in range(2)]) for m in Y_ORDER]


def total_of(part, got):
    return sum([g.astype(F32) for g in got], part)


def on_device(q, k, v, do, doc_lengths):
    own = lax.axis_index("ctx")
    c = own % 2
    core0 = c == 0
    info = jnp.stack([own, c]).astype(jnp.int32)
    ends = jnp.cumsum(doc_lengths).astype(jnp.int32)
    blocks = own + jnp.arange(8, dtype=jnp.int32)
    pos = blocks[:, None] * TOK + jnp.arange(TOK, dtype=jnp.int32)[None, :]
    starts = jnp.max(jnp.where(ends[:, None, None] <= pos[None], ends[:, None, None], 0), axis=0)
    lo = jnp.where(blocks[:, None] < NCTX, jnp.maximum(starts, PROMPT), FAR)

    tok, rows8, prompt, pair = (TOK, WIDE), (8, TOK), (PROMPT, WIDE), (2 * TOK, WIDE)
    turned = (WIDE, TOK)
    smem = pl.BlockSpec(memory_space=pltpu.SMEM)
    vmem = pl.BlockSpec(memory_space=pltpu.VMEM)
    anywhere = pl.BlockSpec(memory_space=pl.ANY)
    kv, qd, sel, held = pl.pallas_call(
        pack_kernel,
        out_shape=[jax.ShapeDtypeStruct(s, BF16) for s in (pair, pair, pair, (2 * PROMPT, WIDE))],
        in_specs=[smem] + [anywhere] * 4,
        out_specs=[vmem] * 4,
        scratch_shapes=[pltpu.SemaphoreType.DMA((4,))],
    )(info, k, v, q, do)

    kv2, qd2 = shift(kv, 2), shift(qd, -2)
    first = swap(sel)
    stat, acc, do_t = call(
        own_kernel, [(rows8, F32), (turned, F32), (turned, F32)], 1, 140_000_000, info, lo, q, k, v, do
    )
    if SPREAD_GATE:
        held, first = lax.optimization_barrier((held, first))
    held = spread(held, own, SPREAD[:2])
    second = jnp.where(core0, qd2, kv2)
    kv2, qd2, first, second, held, stat, acc, do_t = lax.optimization_barrier(
        (kv2, qd2, first, second, held, stat, acc, do_t)
    )

    held = spread(held, own, SPREAD[2:])
    second, kv3, qd3 = swap(second), shift(kv2, 1), shift(qd2, -1)
    kvp = jnp.where(core0, held, swap(held))
    stat, acc = call(
        near_kernel, [(rows8, F32), (turned, F32)], 1, 280_000_000,
        info, lo, stat, acc, q, second, first, kv2,
    )
    if HALO_DONE:
        kv3, qd3, stat, acc = lax.optimization_barrier((kv3, qd3, stat, acc))
    out_t, rows, pk, pv = call(
        last_kernel, [(turned, F32), (rows8, F32), (prompt, BF16), (prompt, BF16)], 1, 300_000_000,
        info, lo, stat, acc, q, do, do_t, kv3, kvp,
    )

    part = gather_cores(pk, pv, c)
    part = total_of(part, gather_z(part.astype(BF16)))
    sent = part.astype(BF16)
    rows_sent, rows_used = rows, rows
    if GATE_R:
        sent, rows_sent = lax.optimization_barrier((sent, rows_sent))
    if GATE_DQ:
        sent, rows_used = lax.optimization_barrier((sent, rows_used))
    got = gather_y(sent)
    r1, r2, r3 = shift(rows_sent, -1), shift(rows_sent, -2), shift(rows_sent, -3)
    att, dq, dk, dv = call(
        query_grad_kernel, [(tok, F32)] * 4, 1, 1_000_000_000,
        info, lo, rows_used, out_t, q, do, k, v, second, first, kv2, kv3, kvp,
    )
    if GATE_Y:
        got[0], dq, att = lax.optimization_barrier((got[0], dq, att))
    part = total_of(part, got)
    if GATE_DK:
        part, r1, r2, r3 = lax.optimization_barrier((part, r1, r2, r3))
    dk, dv, dk_top, dv_top = call(
        key_grad_kernel, [(tok, F32), (tok, F32), (prompt, F32), (prompt, F32)], 1, 900_000_000,
        info, lo, r1, r2, r3, dk, dv, k, v, first, second, qd2, qd3,
    )
    other = swap(part.astype(BF16))
    dk, dv = pl.pallas_call(
        finish_kernel,
        out_shape=[jax.ShapeDtypeStruct(tok, F32)] * 2,
        in_specs=[smem] + [vmem] * 4 + [anywhere] * 2,
        out_specs=[anywhere] * 2,
        scratch_shapes=[pltpu.VMEM(prompt, F32), pltpu.VMEM(prompt, F32), pltpu.SemaphoreType.DMA((2,))],
        input_output_aliases={5: 0, 6: 1},
        compiler_params=pltpu.CompilerParams(vmem_limit_bytes=VMEM_LIMIT),
    )(info, part, other, dk_top, dv_top, dk, dv)
    return att, dq, dk, dv


def solution(mesh):
    spec = P("ctx", "head")
    return jax.shard_map(
        on_device, mesh=mesh, in_specs=(spec,) * 4 + (P(),), out_specs=(spec,) * 4, check_vma=False
    )
```

```python
import math

import jax
import jax.numpy as jnp
from jax import lax
from jax.experimental import pallas as pl
from jax.experimental.pallas import tpu as pltpu
from jax.sharding import PartitionSpec as P

HD = 128
PROMPT = 64
TOK = 256
NCTX = 64
HEADS = 4
WIDE = HEADS * HD
SCALE = 1.0 / math.sqrt(HD)
SCALE2 = SCALE * math.log2(math.e)
NEG = -1e30
FAR = 1 << 28
F32 = jnp.float32
BF16 = jnp.bfloat16
VMEM_LIMIT = 40 * 1024 * 1024
R_AT = "sent"
DK_WINDOW = False
QD_WRAP = True
KV_WRAP = True
GATE_Z = True
GATE_Y2 = False
GATE_DK = True
SPREAD_GATE = True
HALO_DONE = True
Y_FILL = True
Z_FILL = True
Y_STEPS_FILL = False


def mm_nt(a, b):
    return lax.dot_general(a, b, (((1,), (1,)), ((), ())), preferred_element_type=F32)


def mm_nn(a, b):
    return lax.dot_general(a, b, (((1,), (0,)), ((), ())), preferred_element_type=F32)


def mm_tn(a, b):
    return lax.dot_general(a, b, (((0,), (0,)), ((), ())), preferred_element_type=F32)


def head(h):
    return pl.ds(h * HD, HD)


def key_index(base, count):
    return base + lax.broadcasted_iota(jnp.int32, (count, TOK), 0)


def query_index(own):
    return own * TOK + lax.broadcasted_iota(jnp.int32, (1, TOK), 1)


def fold(state, qh, tiles):
    top, total, acc = state
    scores = [jnp.where(ok, mm_nt(kk, qh) * SCALE2, NEG) for ok, kk, _ in tiles]
    new_top = top
    for s in scores:
        new_top = jnp.maximum(new_top, jnp.max(s, axis=0, keepdims=True))
    fade = jnp.exp2(top - new_top)
    total = total * fade
    acc = acc * fade
    for s, (_, _, vv) in zip(scores, tiles):
        p = jnp.exp2(s - new_top)
        total = total + jnp.sum(p, axis=0, keepdims=True)
        acc = acc + mm_tn(vv, p.astype(BF16))
    return (new_top, total, acc), scores


def load_state(stat, acc, h):
    return stat[h : h + 1, :], stat[HEADS + h : HEADS + h + 1, :], acc[head(h), :]


def store_state(stat, acc, h, state):
    stat[h : h + 1, :], stat[HEADS + h : HEADS + h + 1, :], acc[head(h), :] = state


def pack_kernel(info, k, v, q, do, kv, qd, sel, kvp, sems):
    top, bottom = pl.ds(0, TOK), pl.ds(TOK, TOK)
    jobs = [(k, kv.at[top]), (v, kv.at[bottom]), (q, qd.at[top]), (do, qd.at[bottom])]
    copies = [pltpu.make_async_copy(a, b, sems.at[i]) for i, (a, b) in enumerate(jobs)]
    for copy in copies:
        copy.start()
    copies[0].wait()
    copies[1].wait()
    kvp[:PROMPT, :] = kv[:PROMPT, :]
    kvp[PROMPT:, :] = kv[pl.ds(TOK, PROMPT), :]
    copies[2].wait()
    copies[3].wait()
    sel[...] = jnp.where(info[1] == 0, kv[...], qd[...])


def own_kernel(info, lo_ref, q, k, v, do, stat, acc, do_t):
    own = info[0]
    k_pos = key_index(own * TOK, TOK)
    ok = (k_pos >= lo_ref[0:1, :]) & (k_pos <= query_index(own))
    for h in range(HEADS):
        c = head(h)
        start = (jnp.full((1, TOK), NEG, F32), jnp.zeros((1, TOK), F32), jnp.zeros((HD, TOK), F32))
        state, _ = fold(start, q[:, c], [(ok, k[:, c], v[:, c])])
        store_state(stat, acc, h, state)
        do_t[c, :] = jnp.transpose(do[:, c].astype(F32))


def near_kernel(info, lo_ref, stat_in, acc_in, q, kv1a, kv1b, kv2, stat, acc):
    own = info[0]
    core0 = info[1] == 0
    ok1 = key_index((own - 1) * TOK, TOK) >= lo_ref[0:1, :]
    ok2 = key_index((own - 2) * TOK, TOK) >= lo_ref[0:1, :]
    for h in range(HEADS):
        c = head(h)
        kk = jnp.where(core0, kv1a[:TOK, c], kv1b[:TOK, c])
        vv = jnp.where(core0, kv1a[TOK:, c], kv1b[TOK:, c])
        tiles = [(ok1, kk, vv), (ok2, kv2[:TOK, c], kv2[TOK:, c])]
        state, _ = fold(load_state(stat_in, acc_in, h), q[:, c], tiles)
        store_state(stat, acc, h, state)


def last_kernel(info, lo_ref, stat, acc, q, do, do_t, kv3, kvp, out_t, rows, pk, pv):
    own = info[0]
    ok3 = key_index((own - 3) * TOK, TOK) >= lo_ref[0:1, :]
    okp = key_index(0, PROMPT) <= query_index(own)
    dprobs = [mm_nt(kvp[PROMPT:, head(h)], do[:, head(h)]) for h in range(HEADS)]
    folded = []
    for h in range(HEADS):
        c = head(h)
        tiles = [(ok3, kv3[:TOK, c], kv3[TOK:, c]), (okp, kvp[:PROMPT, c], kvp[PROMPT:, c])]
        folded.append(fold(load_state(stat, acc, h), q[:, c], tiles))
    for h in range(HEADS):
        c = head(h)
        (top, total, done), scores = folded[h]
        out = done * (1.0 / total)
        lse = top + jnp.log2(total)
        delta = jnp.sum(out * do_t[c, :], axis=0, keepdims=True)
        out_t[c, :] = out
        rows[h : h + 1, :] = lse
        rows[HEADS + h : HEADS + h + 1, :] = delta
        p = jnp.exp2(scores[1] - lse)
        ds = (p * (dprobs[h] - delta)).astype(BF16)
        pv[:, c] = mm_nn(p.astype(BF16), do[:, c]).astype(BF16)
        pk[:, c] = (mm_nn(ds, q[:, c]) * SCALE).astype(BF16)


def grads(ok, kk, vv, qh, doh, lse, delta):
    p = jnp.where(ok, jnp.exp2(mm_nt(kk, qh) * SCALE2 - lse), 0.0)
    ds = p * (mm_nt(vv, doh) - delta)
    return p.astype(BF16), ds.astype(BF16)


def query_grad_kernel(
    info, lo_ref, rows, out_t, q, do, k, v, kv1a, kv1b, kv2, kv3, kvp, att, dq, dk, dv, acc
):
    own = info[0]
    low = lo_ref[0:1, :]
    q_pos = query_index(own)

    def add(h, ok, kk, vv):
        c = head(h)
        lse, delta = rows[h : h + 1, :], rows[HEADS + h : HEADS + h + 1, :]
        p, ds = grads(ok, kk, vv, q[:, c], do[:, c], lse, delta)
        return p, ds, mm_tn(kk, ds)

    k_pos = key_index(own * TOK, TOK)
    ok_own = (k_pos >= low) & (k_pos <= q_pos)
    ok_prompt = key_index(0, PROMPT) <= q_pos
    for h in range(HEADS):
        c = head(h)
        p, ds, mine = add(h, ok_own, k[:, c], v[:, c])
        dk[:, c] = mm_nn(ds, q[:, c])
        dv[:, c] = mm_nn(p, do[:, c])
        _, _, other = add(h, ok_prompt, kvp[:PROMPT, c], kvp[PROMPT:, c])
        acc[c, :] = mine + other
        att[:, c] = jnp.transpose(out_t[c, :])

    def tile(d, source):
        @pl.when(info[2] < (own - d + 1) * TOK)
        def _():
            ok = key_index((own - d) * TOK, TOK) >= low
            for h in range(HEADS):
                c = head(h)
                acc[c, :] += add(h, ok, source(pl.ds(0, TOK), c), source(pl.ds(TOK, TOK), c))[2]

    tile(1, lambda r, c: jnp.where(info[1] == 0, kv1a[r, c], kv1b[r, c]))
    tile(2, lambda r, c: kv2[r, c])
    tile(3, lambda r, c: kv3[r, c])
    for h in range(HEADS):
        c = head(h)
        dq[:, c] = jnp.transpose(acc[c, :] * SCALE)


def key_grad_kernel(
    info, lo_ref, r1, r2, r3, dk_own, dv_own, k, v, qd1a, qd1b, qd2, qd3, dk, dv, dk_top, dv_top, dk_acc, dv_acc
):
    own = info[0]
    k_pos = key_index(own * TOK, TOK)
    dk_acc[...] = dk_own[...]
    dv_acc[...] = dv_own[...]

    def tile(d, r, source):
        @pl.when(info[2 + d] < (own + 1) * TOK)
        def _():
            ok = k_pos >= lo_ref[d : d + 1, :]
            for h in range(HEADS):
                c = head(h)
                qq, dd = source(pl.ds(0, TOK), c), source(pl.ds(TOK, TOK), c)
                lse, delta = r[h : h + 1, :], r[HEADS + h : HEADS + h + 1, :]
                p, ds = grads(ok, k[:, c], v[:, c], qq, dd, lse, delta)
                dk_acc[:, c] += mm_nn(ds, qq)
                dv_acc[:, c] += mm_nn(p, dd)

    tile(1, r1, lambda r, c: jnp.where(info[1] == 0, qd1a[r, c], qd1b[r, c]))
    tile(2, r2, lambda r, c: qd2[r, c])
    tile(3, r3, lambda r, c: qd3[r, c])
    dk[...] = dk_acc[...] * SCALE
    dv[...] = dv_acc[...]
    dk_top[...] = dk_acc[:PROMPT, :] * SCALE
    dv_top[...] = dv_acc[:PROMPT, :]


def finish_kernel(info, part, other, dk_top, dv_top, dk_in, dv_in, dk, dv, dk_buf, dv_buf, sems):
    first = info[0] == 0
    dk_buf[...] = dk_top[...] + jnp.where(first, part[...], 0.0)
    dv_buf[...] = dv_top[...] + jnp.where(first, other[...].astype(F32), 0.0)
    rows = pl.ds(0, PROMPT)
    copies = [
        pltpu.make_async_copy(dk_buf, dk.at[rows], sems.at[0]),
        pltpu.make_async_copy(dv_buf, dv.at[rows], sems.at[1]),
    ]
    for copy in copies:
        copy.start()
    for copy in copies:
        copy.wait()


def call(kernel, outs, scalars, flops, *args, scratch=()):
    smem = pl.BlockSpec(memory_space=pltpu.SMEM)
    vmem = pl.BlockSpec(memory_space=pltpu.VMEM)
    return pl.pallas_call(
        kernel,
        out_shape=[jax.ShapeDtypeStruct(s, t) for s, t in outs],
        in_specs=[smem] * scalars + [vmem] * (len(args) - scalars),
        out_specs=[vmem] * len(outs),
        scratch_shapes=list(scratch),
        compiler_params=pltpu.CompilerParams(vmem_limit_bytes=VMEM_LIMIT),
        cost_estimate=pl.CostEstimate(flops=flops, bytes_accessed=4 << 20, transcendentals=1 << 20),
    )(*args)


def shift(x, by):
    return lax.ppermute(x, "ctx", [(i, (i + by) % NCTX) for i in range(NCTX)])


def slide(x, by, wrap):
    if wrap:
        return shift(x, by)
    return lax.ppermute(x, "ctx", [(i, i + by) for i in range(NCTX) if 0 <= i + by < NCTX])


def swap(x):
    return lax.ppermute(x, "ctx", [(i, i ^ 1) for i in range(NCTX)])


def at(y, z, c):
    return (y * 8 + z) * 2 + c


def deliver(x, pairs):
    return lax.ppermute(x, "ctx", pairs)


def exchange(x, pairs):
    to = {i: i ^ 1 for i in range(NCTX)}
    for a, b in pairs:
        to[a], to[b] = b, a
    return lax.ppermute(x, "ctx", sorted(to.items()))


Z_ORDER = (4, 5, 3, 6, 2, 7, 1)
Y_ORDER = (2, 3, 1)
SPREAD = (
    ([(at(0, 0, 0), at(0, 4, 0))],),
    tuple([(at(0, n, 0), at(0, n + k, 0)) for n in (0, 4)] for k in (3, 2, 1)),
    tuple([(at(0, n, 0), at(k, n, 0)) for n in range(8)] for k in Y_ORDER),
)


def spread(held, own, steps):
    for step in steps:
        got = [deliver(held, pairs) for pairs in step]
        for pairs, g in zip(step, got):
            takes = sum([own == b for _, b in pairs], jnp.int32(0)) > 0
            held = jnp.where(takes, g, held)
    return held


def gather_cores(pk, pv, c):
    other = swap(jnp.where(c == 0, pv, pk))
    return jnp.where(c == 0, pk, pv).astype(F32) + other.astype(F32)


def gather_z(part):
    route = exchange if Z_FILL else deliver
    return [
        route(part, [(at(m, n, i), at(m, 0, i)) for m in range(4) for i in range(2)]) for n in Z_ORDER
    ]


def gather_y(part):
    route = exchange if Y_FILL else deliver
    return [route(part, [(at(m, 0, i), at(0, 0, i)) for i in range(2)]) for m in Y_ORDER]


def total_of(part, got):
    return sum([g.astype(F32) for g in got], part)


def on_device(q, k, v, do, doc_lengths):
    own = lax.axis_index("ctx")
    c = own % 2
    core0 = c == 0
    ends = jnp.cumsum(doc_lengths).astype(jnp.int32)
    blocks = own + jnp.arange(8, dtype=jnp.int32)
    pos = blocks[:, None] * TOK + jnp.arange(TOK, dtype=jnp.int32)[None, :]
    starts = jnp.max(jnp.where(ends[:, None, None] <= pos[None], ends[:, None, None], 0), axis=0)
    lo = jnp.where(blocks[:, None] < NCTX, jnp.maximum(starts, PROMPT), FAR)

    info = jnp.concatenate([jnp.stack([own, c]).astype(jnp.int32), lo[:4, 0]])
    place = jnp.stack([own, c]).astype(jnp.int32)

    tok, rows8, prompt, pair = (TOK, WIDE), (8, TOK), (PROMPT, WIDE), (2 * TOK, WIDE)
    turned = (WIDE, TOK)
    smem = pl.BlockSpec(memory_space=pltpu.SMEM)
    vmem = pl.BlockSpec(memory_space=pltpu.VMEM)
    anywhere = pl.BlockSpec(memory_space=pl.ANY)
    kv, qd, sel, held = pl.pallas_call(
        pack_kernel,
        out_shape=[jax.ShapeDtypeStruct(s, BF16) for s in (pair, pair, pair, (2 * PROMPT, WIDE))],
        in_specs=[smem] + [anywhere] * 4,
        out_specs=[vmem] * 4,
        scratch_shapes=[pltpu.SemaphoreType.DMA((4,))],
    )(place, k, v, q, do)

    kv2, qd2 = slide(kv, 2, KV_WRAP), slide(qd, -2, QD_WRAP)
    first = swap(sel)
    stat, acc, do_t = call(
        own_kernel, [(rows8, F32), (turned, F32), (turned, F32)], 1, 140_000_000, info, lo, q, k, v, do
    )
    if SPREAD_GATE:
        held, first = lax.optimization_barrier((held, first))
    held = spread(held, own, SPREAD[:2])
    second = jnp.where(core0, qd2, kv2)
    kv2, qd2, first, second, held, stat, acc, do_t = lax.optimization_barrier(
        (kv2, qd2, first, second, held, stat, acc, do_t)
    )

    second, kv3, qd3 = swap(second), slide(kv2, 1, KV_WRAP), slide(qd2, -1, QD_WRAP)
    if GATE_Y2:
        held, second = lax.optimization_barrier((held, second))
    held = spread(held, own, SPREAD[2:])
    kvp = jnp.where(core0, held, swap(held))
    stat, acc = call(
        near_kernel, [(rows8, F32), (turned, F32)], 1, 280_000_000,
        info, lo, stat, acc, q, second, first, kv2,
    )
    if HALO_DONE:
        kv3, qd3, stat, acc = lax.optimization_barrier((kv3, qd3, stat, acc))
    out_t, rows, pk, pv = call(
        last_kernel, [(turned, F32), (rows8, F32), (prompt, BF16), (prompt, BF16)], 1, 300_000_000,
        info, lo, stat, acc, q, do, do_t, kv3, kvp,
    )

    part = gather_cores(pk, pv, c)
    rows_sent = rows
    if R_AT == "part":
        part, rows_sent = lax.optimization_barrier((part, rows_sent))
    got = gather_z(part.astype(BF16))
    if R_AT == "got":
        got[6], rows_sent = lax.optimization_barrier((got[6], rows_sent))
    att, dq, dk, dv = call(
        query_grad_kernel, [(tok, F32)] * 4, 1, 1_000_000_000,
        info, lo, rows, out_t, q, do, k, v, second, first, kv2, kv3, kvp,
        scratch=[pltpu.VMEM(turned, F32)],
    )
    if GATE_Z:
        got[0], att, dq, dk, dv = lax.optimization_barrier((got[0], att, dq, dk, dv))
    part = total_of(part, got)
    sent = part.astype(BF16)
    if R_AT == "sent":
        sent, rows_sent = lax.optimization_barrier((sent, rows_sent))
    r1, r2, r3 = shift(rows_sent, -1), shift(rows_sent, -2), shift(rows_sent, -3)
    if DK_WINDOW:
        sent, r1, r2, r3 = lax.optimization_barrier((sent, r1, r2, r3))
    got = gather_y(sent)
    if not DK_WINDOW:
        part = total_of(part, got)
        if GATE_DK:
            part, r1, r2, r3 = lax.optimization_barrier((part, r1, r2, r3))
    dk, dv, dk_top, dv_top = call(
        key_grad_kernel, [(tok, F32), (tok, F32), (prompt, F32), (prompt, F32)], 1, 900_000_000,
        info, lo, r1, r2, r3, dk, dv, k, v, first, second, qd2, qd3,
        scratch=[pltpu.VMEM(tok, F32), pltpu.VMEM(tok, F32)],
    )
    if DK_WINDOW:
        got[0], dk, dv = lax.optimization_barrier((got[0], dk, dv))
        part = total_of(part, got)
    other = swap(part.astype(BF16))
    dk, dv = pl.pallas_call(
        finish_kernel,
        out_shape=[jax.ShapeDtypeStruct(tok, F32)] * 2,
        in_specs=[smem] + [vmem] * 4 + [anywhere] * 2,
        out_specs=[anywhere] * 2,
        scratch_shapes=[pltpu.VMEM(prompt, F32), pltpu.VMEM(prompt, F32), pltpu.SemaphoreType.DMA((2,))],
        input_output_aliases={5: 0, 6: 1},
        compiler_params=pltpu.CompilerParams(vmem_limit_bytes=VMEM_LIMIT),
    )(info, part, other, dk_top, dv_top, dk, dv)
    return att, dq, dk, dv


def solution(mesh):
    spec = P("ctx", "head")
    return jax.shard_map(
        on_device, mesh=mesh, in_specs=(spec,) * 4 + (P(),), out_specs=(spec,) * 4, check_vma=False
    )
```

```python
import math

import jax
import jax.numpy as jnp
from jax import lax
from jax.experimental import pallas as pl
from jax.experimental.pallas import tpu as pltpu
from jax.sharding import PartitionSpec as P

HD = 128
PROMPT = 64
TOK = 256
NCTX = 64
HEADS = 4
WIDE = HEADS * HD
SCALE = 1.0 / math.sqrt(HD)
SCALE2 = SCALE * math.log2(math.e)
NEG = -1e30
FAR = 1 << 28
F32 = jnp.float32
BF16 = jnp.bfloat16
VMEM_LIMIT = 40 * 1024 * 1024
R_AT = "sent"
FAN = ((2, 6), (7, 3), (1, 5))
DK_WINDOW = False
QD_WRAP = True
KV_WRAP = True
GATE_Z = True
GATE_Y2 = False
GATE_DK = True
SPREAD_GATE = True
HALO_DONE = True
Y_FILL = True
Z_FILL = True
Y_STEPS_FILL = False


def mm_nt(a, b):
    return lax.dot_general(a, b, (((1,), (1,)), ((), ())), preferred_element_type=F32)


def mm_nn(a, b):
    return lax.dot_general(a, b, (((1,), (0,)), ((), ())), preferred_element_type=F32)


def mm_tn(a, b):
    return lax.dot_general(a, b, (((0,), (0,)), ((), ())), preferred_element_type=F32)


def head(h):
    return pl.ds(h * HD, HD)


def key_index(base, count):
    return base + lax.broadcasted_iota(jnp.int32, (count, TOK), 0)


def query_index(own):
    return own * TOK + lax.broadcasted_iota(jnp.int32, (1, TOK), 1)


def fold(state, qh, tiles):
    top, total, acc = state
    scores = [jnp.where(ok, mm_nt(kk, qh) * SCALE2, NEG) for ok, kk, _ in tiles]
    new_top = top
    for s in scores:
        new_top = jnp.maximum(new_top, jnp.max(s, axis=0, keepdims=True))
    fade = jnp.exp2(top - new_top)
    total = total * fade
    acc = acc * fade
    for s, (_, _, vv) in zip(scores, tiles):
        p = jnp.exp2(s - new_top)
        total = total + jnp.sum(p, axis=0, keepdims=True)
        acc = acc + mm_tn(vv, p.astype(BF16))
    return (new_top, total, acc), scores


def load_state(stat, acc, h):
    return stat[h : h + 1, :], stat[HEADS + h : HEADS + h + 1, :], acc[head(h), :]


def store_state(stat, acc, h, state):
    stat[h : h + 1, :], stat[HEADS + h : HEADS + h + 1, :], acc[head(h), :] = state


def pack_kernel(info, k, v, q, do, kv, qd, sel, kvp, sems):
    top, bottom = pl.ds(0, TOK), pl.ds(TOK, TOK)
    jobs = [(k, kv.at[top]), (v, kv.at[bottom]), (q, qd.at[top]), (do, qd.at[bottom])]
    copies = [pltpu.make_async_copy(a, b, sems.at[i]) for i, (a, b) in enumerate(jobs)]
    for copy in copies:
        copy.start()
    copies[0].wait()
    copies[1].wait()
    kvp[:PROMPT, :] = kv[:PROMPT, :]
    kvp[PROMPT:, :] = kv[pl.ds(TOK, PROMPT), :]
    copies[2].wait()
    copies[3].wait()
    sel[...] = jnp.where(info[1] == 0, kv[...], qd[...])


def own_kernel(info, lo_ref, q, k, v, do, stat, acc, do_t):
    own = info[0]
    k_pos = key_index(own * TOK, TOK)
    ok = (k_pos >= lo_ref[0:1, :]) & (k_pos <= query_index(own))
    for h in range(HEADS):
        c = head(h)
        start = (jnp.full((1, TOK), NEG, F32), jnp.zeros((1, TOK), F32), jnp.zeros((HD, TOK), F32))
        state, _ = fold(start, q[:, c], [(ok, k[:, c], v[:, c])])
        store_state(stat, acc, h, state)
        do_t[c, :] = jnp.transpose(do[:, c].astype(F32))


def near_kernel(info, lo_ref, stat_in, acc_in, q, kv1a, kv1b, kv2, stat, acc):
    own = info[0]
    core0 = info[1] == 0
    ok1 = key_index((own - 1) * TOK, TOK) >= lo_ref[0:1, :]
    ok2 = key_index((own - 2) * TOK, TOK) >= lo_ref[0:1, :]
    for h in range(HEADS):
        c = head(h)
        kk = jnp.where(core0, kv1a[:TOK, c], kv1b[:TOK, c])
        vv = jnp.where(core0, kv1a[TOK:, c], kv1b[TOK:, c])
        tiles = [(ok1, kk, vv), (ok2, kv2[:TOK, c], kv2[TOK:, c])]
        state, _ = fold(load_state(stat_in, acc_in, h), q[:, c], tiles)
        store_state(stat, acc, h, state)


def last_kernel(info, lo_ref, stat, acc, q, do, do_t, kv3, kvp, out_t, rows, pk, pv):
    own = info[0]
    ok3 = key_index((own - 3) * TOK, TOK) >= lo_ref[0:1, :]
    okp = key_index(0, PROMPT) <= query_index(own)
    dprobs = [mm_nt(kvp[PROMPT:, head(h)], do[:, head(h)]) for h in range(HEADS)]
    folded = []
    for h in range(HEADS):
        c = head(h)
        tiles = [(ok3, kv3[:TOK, c], kv3[TOK:, c]), (okp, kvp[:PROMPT, c], kvp[PROMPT:, c])]
        folded.append(fold(load_state(stat, acc, h), q[:, c], tiles))
    for h in range(HEADS):
        c = head(h)
        (top, total, done), scores = folded[h]
        out = done * (1.0 / total)
        lse = top + jnp.log2(total)
        delta = jnp.sum(out * do_t[c, :], axis=0, keepdims=True)
        out_t[c, :] = out
        rows[h : h + 1, :] = lse
        rows[HEADS + h : HEADS + h + 1, :] = delta
        p = jnp.exp2(scores[1] - lse)
        ds = (p * (dprobs[h] - delta)).astype(BF16)
        pv[:, c] = mm_nn(p.astype(BF16), do[:, c]).astype(BF16)
        pk[:, c] = (mm_nn(ds, q[:, c]) * SCALE).astype(BF16)


def grads(ok, kk, vv, qh, doh, lse, delta):
    p = jnp.where(ok, jnp.exp2(mm_nt(kk, qh) * SCALE2 - lse), 0.0)
    ds = p * (mm_nt(vv, doh) - delta)
    return p.astype(BF16), ds.astype(BF16)


def query_grad_kernel(
    info, lo_ref, rows, out_t, q, do, k, v, kv1a, kv1b, kv2, kv3, kvp, att, dq, dk, dv, acc
):
    own = info[0]
    low = lo_ref[0:1, :]
    q_pos = query_index(own)

    def add(h, ok, kk, vv):
        c = head(h)
        lse, delta = rows[h : h + 1, :], rows[HEADS + h : HEADS + h + 1, :]
        p, ds = grads(ok, kk, vv, q[:, c], do[:, c], lse, delta)
        return p, ds, mm_tn(kk, ds)

    k_pos = key_index(own * TOK, TOK)
    ok_own = (k_pos >= low) & (k_pos <= q_pos)
    ok_prompt = key_index(0, PROMPT) <= q_pos
    for h in range(HEADS):
        c = head(h)
        p, ds, mine = add(h, ok_own, k[:, c], v[:, c])
        dk[:, c] = mm_nn(ds, q[:, c])
        dv[:, c] = mm_nn(p, do[:, c])
        _, _, other = add(h, ok_prompt, kvp[:PROMPT, c], kvp[PROMPT:, c])
        acc[c, :] = mine + other
        att[:, c] = jnp.transpose(out_t[c, :])

    def tile(d, source):
        @pl.when(info[2] < (own - d + 1) * TOK)
        def _():
            ok = key_index((own - d) * TOK, TOK) >= low
            for h in range(HEADS):
                c = head(h)
                acc[c, :] += add(h, ok, source(pl.ds(0, TOK), c), source(pl.ds(TOK, TOK), c))[2]

    tile(1, lambda r, c: jnp.where(info[1] == 0, kv1a[r, c], kv1b[r, c]))
    tile(2, lambda r, c: kv2[r, c])
    tile(3, lambda r, c: kv3[r, c])
    for h in range(HEADS):
        c = head(h)
        dq[:, c] = jnp.transpose(acc[c, :] * SCALE)


def key_grad_kernel(
    info, lo_ref, r1, r2, r3, dk_own, dv_own, k, v, qd1a, qd1b, qd2, qd3, dk, dv, dk_top, dv_top, dk_acc, dv_acc
):
    own = info[0]
    k_pos = key_index(own * TOK, TOK)
    dk_acc[...] = dk_own[...]
    dv_acc[...] = dv_own[...]

    def tile(d, r, source):
        @pl.when(info[2 + d] < (own + 1) * TOK)
        def _():
            ok = k_pos >= lo_ref[d : d + 1, :]
            for h in range(HEADS):
                c = head(h)
                qq, dd = source(pl.ds(0, TOK), c), source(pl.ds(TOK, TOK), c)
                lse, delta = r[h : h + 1, :], r[HEADS + h : HEADS + h + 1, :]
                p, ds = grads(ok, k[:, c], v[:, c], qq, dd, lse, delta)
                dk_acc[:, c] += mm_nn(ds, qq)
                dv_acc[:, c] += mm_nn(p, dd)

    tile(1, r1, lambda r, c: jnp.where(info[1] == 0, qd1a[r, c], qd1b[r, c]))
    tile(2, r2, lambda r, c: qd2[r, c])
    tile(3, r3, lambda r, c: qd3[r, c])
    dk[...] = dk_acc[...] * SCALE
    dv[...] = dv_acc[...]
    dk_top[...] = dk_acc[:PROMPT, :] * SCALE
    dv_top[...] = dv_acc[:PROMPT, :]


def finish_kernel(info, part, other, dk_top, dv_top, dk_in, dv_in, dk, dv, dk_buf, dv_buf, sems):
    first = info[0] == 0
    dk_buf[...] = dk_top[...] + jnp.where(first, part[...], 0.0)
    dv_buf[...] = dv_top[...] + jnp.where(first, other[...].astype(F32), 0.0)
    rows = pl.ds(0, PROMPT)
    copies = [
        pltpu.make_async_copy(dk_buf, dk.at[rows], sems.at[0]),
        pltpu.make_async_copy(dv_buf, dv.at[rows], sems.at[1]),
    ]
    for copy in copies:
        copy.start()
    for copy in copies:
        copy.wait()


def call(kernel, outs, scalars, flops, *args, scratch=()):
    smem = pl.BlockSpec(memory_space=pltpu.SMEM)
    vmem = pl.BlockSpec(memory_space=pltpu.VMEM)
    return pl.pallas_call(
        kernel,
        out_shape=[jax.ShapeDtypeStruct(s, t) for s, t in outs],
        in_specs=[smem] * scalars + [vmem] * (len(args) - scalars),
        out_specs=[vmem] * len(outs),
        scratch_shapes=list(scratch),
        compiler_params=pltpu.CompilerParams(vmem_limit_bytes=VMEM_LIMIT),
        cost_estimate=pl.CostEstimate(flops=flops, bytes_accessed=4 << 20, transcendentals=1 << 20),
    )(*args)


def shift(x, by):
    return lax.ppermute(x, "ctx", [(i, (i + by) % NCTX) for i in range(NCTX)])


def slide(x, by, wrap):
    if wrap:
        return shift(x, by)
    return lax.ppermute(x, "ctx", [(i, i + by) for i in range(NCTX) if 0 <= i + by < NCTX])


def swap(x):
    return lax.ppermute(x, "ctx", [(i, i ^ 1) for i in range(NCTX)])


def at(y, z, c):
    return (y * 8 + z) * 2 + c


def deliver(x, pairs):
    return lax.ppermute(x, "ctx", pairs)


def exchange(x, pairs):
    to = {i: i ^ 1 for i in range(NCTX)}
    for a, b in pairs:
        to[a], to[b] = b, a
    return lax.ppermute(x, "ctx", sorted(to.items()))


Z_ORDER = (1, 7, 2, 6, 3, 5, 4)
Y_ORDER = (2, 3, 1)
SPREAD = (
    ([(at(0, 0, 0), at(0, 4, 0))],),
    tuple([(at(0, 0, 0), at(0, a, 0)), (at(0, 4, 0), at(0, b, 0))] for a, b in FAN),
    tuple([(at(0, n, 0), at(k, n, 0)) for n in range(8)] for k in Y_ORDER),
)


def spread(held, own, steps):
    for step in steps:
        got = [deliver(held, pairs) for pairs in step]
        for pairs, g in zip(step, got):
            takes = sum([own == b for _, b in pairs], jnp.int32(0)) > 0
            held = jnp.where(takes, g, held)
    return held


def gather_cores(pk, pv, c):
    other = swap(jnp.where(c == 0, pv, pk))
    return jnp.where(c == 0, pk, pv).astype(F32) + other.astype(F32)


def gather_z(part):
    route = exchange if Z_FILL else deliver
    return [
        route(part, [(at(m, n, i), at(m, 0, i)) for m in range(4) for i in range(2)]) for n in Z_ORDER
    ]


def gather_y(part):
    route = exchange if Y_FILL else deliver
    return [route(part, [(at(m, 0, i), at(0, 0, i)) for i in range(2)]) for m in Y_ORDER]


def total_of(part, got):
    return sum([g.astype(F32) for g in got], part)


def on_device(q, k, v, do, doc_lengths):
    own = lax.axis_index("ctx")
    c = own % 2
    core0 = c == 0
    ends = jnp.cumsum(doc_lengths).astype(jnp.int32)
    blocks = own + jnp.arange(8, dtype=jnp.int32)
    pos = blocks[:, None] * TOK + jnp.arange(TOK, dtype=jnp.int32)[None, :]
    starts = jnp.max(jnp.where(ends[:, None, None] <= pos[None], ends[:, None, None], 0), axis=0)
    lo = jnp.where(blocks[:, None] < NCTX, jnp.maximum(starts, PROMPT), FAR)

    info = jnp.concatenate([jnp.stack([own, c]).astype(jnp.int32), lo[:4, 0]])
    place = jnp.stack([own, c]).astype(jnp.int32)

    tok, rows8, prompt, pair = (TOK, WIDE), (8, TOK), (PROMPT, WIDE), (2 * TOK, WIDE)
    turned = (WIDE, TOK)
    smem = pl.BlockSpec(memory_space=pltpu.SMEM)
    vmem = pl.BlockSpec(memory_space=pltpu.VMEM)
    anywhere = pl.BlockSpec(memory_space=pl.ANY)
    kv, qd, sel, held = pl.pallas_call(
        pack_kernel,
        out_shape=[jax.ShapeDtypeStruct(s, BF16) for s in (pair, pair, pair, (2 * PROMPT, WIDE))],
        in_specs=[smem] + [anywhere] * 4,
        out_specs=[vmem] * 4,
        scratch_shapes=[pltpu.SemaphoreType.DMA((4,))],
    )(place, k, v, q, do)

    kv2, qd2 = slide(kv, 2, KV_WRAP), slide(qd, -2, QD_WRAP)
    first = swap(sel)
    stat, acc, do_t = call(
        own_kernel, [(rows8, F32), (turned, F32), (turned, F32)], 1, 140_000_000, info, lo, q, k, v, do
    )
    if SPREAD_GATE:
        held, first = lax.optimization_barrier((held, first))
    held = spread(held, own, SPREAD[:2])
    second = jnp.where(core0, qd2, kv2)
    kv2, qd2, first, second, held, stat, acc, do_t = lax.optimization_barrier(
        (kv2, qd2, first, second, held, stat, acc, do_t)
    )

    second, kv3, qd3 = swap(second), slide(kv2, 1, KV_WRAP), slide(qd2, -1, QD_WRAP)
    if GATE_Y2:
        held, second = lax.optimization_barrier((held, second))
    held = spread(held, own, SPREAD[2:])
    kvp = jnp.where(core0, held, swap(held))
    stat, acc = call(
        near_kernel, [(rows8, F32), (turned, F32)], 1, 280_000_000,
        info, lo, stat, acc, q, second, first, kv2,
    )
    if HALO_DONE:
        kv3, qd3, stat, acc = lax.optimization_barrier((kv3, qd3, stat, acc))
    out_t, rows, pk, pv = call(
        last_kernel, [(turned, F32), (rows8, F32), (prompt, BF16), (prompt, BF16)], 1, 300_000_000,
        info, lo, stat, acc, q, do, do_t, kv3, kvp,
    )

    part = gather_cores(pk, pv, c)
    rows_sent = rows
    if R_AT == "part":
        part, rows_sent = lax.optimization_barrier((part, rows_sent))
    got = gather_z(part.astype(BF16))
    if R_AT == "got":
        got[6], rows_sent = lax.optimization_barrier((got[6], rows_sent))
    att, dq, dk, dv = call(
        query_grad_kernel, [(tok, F32)] * 4, 1, 1_000_000_000,
        info, lo, rows, out_t, q, do, k, v, second, first, kv2, kv3, kvp,
        scratch=[pltpu.VMEM(turned, F32)],
    )
    if R_AT == "dq":
        rows_sent = lax.optimization_barrier((rows, dq))[0]
    if GATE_Z:
        got[0], att, dq, dk, dv = lax.optimization_barrier((got[0], att, dq, dk, dv))
    part = total_of(part, got)
    sent = part.astype(BF16)
    if R_AT == "sent":
        sent, rows_sent = lax.optimization_barrier((sent, rows_sent))
    r1, r2, r3 = shift(rows_sent, -1), shift(rows_sent, -2), shift(rows_sent, -3)
    if DK_WINDOW:
        r1 = lax.optimization_barrier((r1, sent))[0]
    got = gather_y(sent)
    if not DK_WINDOW:
        part = total_of(part, got)
        if GATE_DK:
            r1 = lax.optimization_barrier((r1, part))[0]
    dk, dv, dk_top, dv_top = call(
        key_grad_kernel, [(tok, F32), (tok, F32), (prompt, F32), (prompt, F32)], 1, 900_000_000,
        info, lo, r1, r2, r3, dk, dv, k, v, first, second, qd2, qd3,
        scratch=[pltpu.VMEM(tok, F32), pltpu.VMEM(tok, F32)],
    )
    if DK_WINDOW:
        got[0], dk, dv = lax.optimization_barrier((got[0], dk, dv))
        part = total_of(part, got)
    other = swap(part.astype(BF16))
    dk, dv = pl.pallas_call(
        finish_kernel,
        out_shape=[jax.ShapeDtypeStruct(tok, F32)] * 2,
        in_specs=[smem] + [vmem] * 4 + [anywhere] * 2,
        out_specs=[anywhere] * 2,
        scratch_shapes=[pltpu.VMEM(prompt, F32), pltpu.VMEM(prompt, F32), pltpu.SemaphoreType.DMA((2,))],
        input_output_aliases={5: 0, 6: 1},
        compiler_params=pltpu.CompilerParams(vmem_limit_bytes=VMEM_LIMIT),
    )(info, part, other, dk_top, dv_top, dk, dv)
    return att, dq, dk, dv


def solution(mesh):
    spec = P("ctx", "head")
    return jax.shard_map(
        on_device, mesh=mesh, in_specs=(spec,) * 4 + (P(),), out_specs=(spec,) * 4, check_vma=False
    )
```

```python
import math

import jax
import jax.numpy as jnp
from jax import lax
from jax.experimental import pallas as pl
from jax.experimental.pallas import tpu as pltpu
from jax.sharding import PartitionSpec as P

HD = 128
PROMPT = 64
TOK = 256
NCTX = 64
HEADS = 4
WIDE = HEADS * HD
SCALE = 1.0 / math.sqrt(HD)
SCALE2 = SCALE * math.log2(math.e)
NEG = -1e30
FAR = 1 << 28
F32 = jnp.float32
BF16 = jnp.bfloat16
VMEM_LIMIT = 40 * 1024 * 1024
R_AT = "sent"
FAN = ((1, 5), (7, 3), (2, 6))
DK_WINDOW = False
QD_WRAP = True
KV_WRAP = True
GATE_Z = True
GATE_Y2 = False
GATE_DK = True
SPREAD_GATE = True
HALO_DONE = True
Y_FILL = True
Z_FILL = True
Y_STEPS_FILL = False


def mm_nt(a, b):
    return lax.dot_general(a, b, (((1,), (1,)), ((), ())), preferred_element_type=F32)


def mm_nn(a, b):
    return lax.dot_general(a, b, (((1,), (0,)), ((), ())), preferred_element_type=F32)


def mm_tn(a, b):
    return lax.dot_general(a, b, (((0,), (0,)), ((), ())), preferred_element_type=F32)


def head(h):
    return pl.ds(h * HD, HD)


def key_index(base, count):
    return base + lax.broadcasted_iota(jnp.int32, (count, TOK), 0)


def query_index(own):
    return own * TOK + lax.broadcasted_iota(jnp.int32, (1, TOK), 1)


def fold(state, qh, tiles):
    top, total, acc = state
    scores = [jnp.where(ok, mm_nt(kk, qh) * SCALE2, NEG) for ok, kk, _ in tiles]
    new_top = top
    for s in scores:
        new_top = jnp.maximum(new_top, jnp.max(s, axis=0, keepdims=True))
    fade = jnp.exp2(top - new_top)
    total = total * fade
    acc = acc * fade
    for s, (_, _, vv) in zip(scores, tiles):
        p = jnp.exp2(s - new_top)
        total = total + jnp.sum(p, axis=0, keepdims=True)
        acc = acc + mm_tn(vv, p.astype(BF16))
    return (new_top, total, acc), scores


def load_state(stat, acc, h):
    return stat[h : h + 1, :], stat[HEADS + h : HEADS + h + 1, :], acc[head(h), :]


def store_state(stat, acc, h, state):
    stat[h : h + 1, :], stat[HEADS + h : HEADS + h + 1, :], acc[head(h), :] = state


def pack_kernel(info, k, v, q, do, kv, qd, sel, kvp, sems):
    top, bottom = pl.ds(0, TOK), pl.ds(TOK, TOK)
    jobs = [(k, kv.at[top]), (v, kv.at[bottom]), (q, qd.at[top]), (do, qd.at[bottom])]
    copies = [pltpu.make_async_copy(a, b, sems.at[i]) for i, (a, b) in enumerate(jobs)]
    for copy in copies:
        copy.start()
    copies[0].wait()
    copies[1].wait()
    kvp[:PROMPT, :] = kv[:PROMPT, :]
    kvp[PROMPT:, :] = kv[pl.ds(TOK, PROMPT), :]
    copies[2].wait()
    copies[3].wait()
    sel[...] = jnp.where(info[1] == 0, kv[...], qd[...])


def own_kernel(info, lo_ref, q, k, v, do, stat, acc, do_t):
    own = info[0]
    k_pos = key_index(own * TOK, TOK)
    ok = (k_pos >= lo_ref[0:1, :]) & (k_pos <= query_index(own))
    for h in range(HEADS):
        c = head(h)
        start = (jnp.full((1, TOK), NEG, F32), jnp.zeros((1, TOK), F32), jnp.zeros((HD, TOK), F32))
        state, _ = fold(start, q[:, c], [(ok, k[:, c], v[:, c])])
        store_state(stat, acc, h, state)
        do_t[c, :] = jnp.transpose(do[:, c].astype(F32))


def near_kernel(info, lo_ref, stat_in, acc_in, q, kv1a, kv1b, kv2, stat, acc):
    own = info[0]
    core0 = info[1] == 0
    ok1 = key_index((own - 1) * TOK, TOK) >= lo_ref[0:1, :]
    ok2 = key_index((own - 2) * TOK, TOK) >= lo_ref[0:1, :]
    for h in range(HEADS):
        c = head(h)
        kk = jnp.where(core0, kv1a[:TOK, c], kv1b[:TOK, c])
        vv = jnp.where(core0, kv1a[TOK:, c], kv1b[TOK:, c])
        tiles = [(ok1, kk, vv), (ok2, kv2[:TOK, c], kv2[TOK:, c])]
        state, _ = fold(load_state(stat_in, acc_in, h), q[:, c], tiles)
        store_state(stat, acc, h, state)


def last_kernel(info, lo_ref, stat, acc, q, do, do_t, kv3, kvp, out_t, rows, pk, pv):
    own = info[0]
    ok3 = key_index((own - 3) * TOK, TOK) >= lo_ref[0:1, :]
    okp = key_index(0, PROMPT) <= query_index(own)
    dprobs = [mm_nt(kvp[PROMPT:, head(h)], do[:, head(h)]) for h in range(HEADS)]
    folded = []
    for h in range(HEADS):
        c = head(h)
        tiles = [(ok3, kv3[:TOK, c], kv3[TOK:, c]), (okp, kvp[:PROMPT, c], kvp[PROMPT:, c])]
        folded.append(fold(load_state(stat, acc, h), q[:, c], tiles))
    for h in range(HEADS):
        c = head(h)
        (top, total, done), scores = folded[h]
        out = done * (1.0 / total)
        lse = top + jnp.log2(total)
        delta = jnp.sum(out * do_t[c, :], axis=0, keepdims=True)
        out_t[c, :] = out
        rows[h : h + 1, :] = lse
        rows[HEADS + h : HEADS + h + 1, :] = delta
        p = jnp.exp2(scores[1] - lse)
        ds = (p * (dprobs[h] - delta)).astype(BF16)
        pv[:, c] = mm_nn(p.astype(BF16), do[:, c]).astype(BF16)
        pk[:, c] = (mm_nn(ds, q[:, c]) * SCALE).astype(BF16)


def grads(ok, kk, vv, qh, doh, lse, delta):
    p = jnp.where(ok, jnp.exp2(mm_nt(kk, qh) * SCALE2 - lse), 0.0)
    ds = p * (mm_nt(vv, doh) - delta)
    return p.astype(BF16), ds.astype(BF16)


def query_grad_kernel(
    info, lo_ref, rows, out_t, q, do, k, v, kv1a, kv1b, kv2, kv3, kvp, att, dq, dk, dv, acc
):
    own = info[0]
    low = lo_ref[0:1, :]
    q_pos = query_index(own)

    def add(h, ok, kk, vv):
        c = head(h)
        lse, delta = rows[h : h + 1, :], rows[HEADS + h : HEADS + h + 1, :]
        p, ds = grads(ok, kk, vv, q[:, c], do[:, c], lse, delta)
        return p, ds, mm_tn(kk, ds)

    k_pos = key_index(own * TOK, TOK)
    ok_own = (k_pos >= low) & (k_pos <= q_pos)
    ok_prompt = key_index(0, PROMPT) <= q_pos
    for h in range(HEADS):
        c = head(h)
        p, ds, mine = add(h, ok_own, k[:, c], v[:, c])
        dk[:, c] = mm_nn(ds, q[:, c])
        dv[:, c] = mm_nn(p, do[:, c])
        _, _, other = add(h, ok_prompt, kvp[:PROMPT, c], kvp[PROMPT:, c])
        acc[c, :] = mine + other
        att[:, c] = jnp.transpose(out_t[c, :])

    def tile(d, source):
        @pl.when(info[2] < (own - d + 1) * TOK)
        def _():
            ok = key_index((own - d) * TOK, TOK) >= low
            for h in range(HEADS):
                c = head(h)
                acc[c, :] += add(h, ok, source(pl.ds(0, TOK), c), source(pl.ds(TOK, TOK), c))[2]

    tile(1, lambda r, c: jnp.where(info[1] == 0, kv1a[r, c], kv1b[r, c]))
    tile(2, lambda r, c: kv2[r, c])
    tile(3, lambda r, c: kv3[r, c])
    for h in range(HEADS):
        c = head(h)
        dq[:, c] = jnp.transpose(acc[c, :] * SCALE)


def key_grad_kernel(
    info, lo_ref, r1, r2, r3, dk_own, dv_own, k, v, qd1a, qd1b, qd2, qd3, dk, dv, dk_top, dv_top, dk_acc, dv_acc
):
    own = info[0]
    k_pos = key_index(own * TOK, TOK)
    dk_acc[...] = dk_own[...]
    dv_acc[...] = dv_own[...]

    def tile(d, r, source):
        @pl.when(info[2 + d] < (own + 1) * TOK)
        def _():
            ok = k_pos >= lo_ref[d : d + 1, :]
            for h in range(HEADS):
                c = head(h)
                qq, dd = source(pl.ds(0, TOK), c), source(pl.ds(TOK, TOK), c)
                lse, delta = r[h : h + 1, :], r[HEADS + h : HEADS + h + 1, :]
                p, ds = grads(ok, k[:, c], v[:, c], qq, dd, lse, delta)
                dk_acc[:, c] += mm_nn(ds, qq)
                dv_acc[:, c] += mm_nn(p, dd)

    tile(1, r1, lambda r, c: jnp.where(info[1] == 0, qd1a[r, c], qd1b[r, c]))
    tile(2, r2, lambda r, c: qd2[r, c])
    tile(3, r3, lambda r, c: qd3[r, c])
    dk[...] = dk_acc[...] * SCALE
    dv[...] = dv_acc[...]
    dk_top[...] = dk_acc[:PROMPT, :] * SCALE
    dv_top[...] = dv_acc[:PROMPT, :]


def finish_kernel(info, part, other, dk_top, dv_top, dk_in, dv_in, dk, dv, dk_buf, dv_buf, sems):
    first = info[0] == 0
    dk_buf[...] = dk_top[...] + jnp.where(first, part[...], 0.0)
    dv_buf[...] = dv_top[...] + jnp.where(first, other[...].astype(F32), 0.0)
    rows = pl.ds(0, PROMPT)
    copies = [
        pltpu.make_async_copy(dk_buf, dk.at[rows], sems.at[0]),
        pltpu.make_async_copy(dv_buf, dv.at[rows], sems.at[1]),
    ]
    for copy in copies:
        copy.start()
    for copy in copies:
        copy.wait()


def call(kernel, outs, scalars, flops, *args, scratch=()):
    smem = pl.BlockSpec(memory_space=pltpu.SMEM)
    vmem = pl.BlockSpec(memory_space=pltpu.VMEM)
    return pl.pallas_call(
        kernel,
        out_shape=[jax.ShapeDtypeStruct(s, t) for s, t in outs],
        in_specs=[smem] * scalars + [vmem] * (len(args) - scalars),
        out_specs=[vmem] * len(outs),
        scratch_shapes=list(scratch),
        compiler_params=pltpu.CompilerParams(vmem_limit_bytes=VMEM_LIMIT),
        cost_estimate=pl.CostEstimate(flops=flops, bytes_accessed=4 << 20, transcendentals=1 << 20),
    )(*args)


def shift(x, by):
    return lax.ppermute(x, "ctx", [(i, (i + by) % NCTX) for i in range(NCTX)])


def slide(x, by, wrap):
    if wrap:
        return shift(x, by)
    return lax.ppermute(x, "ctx", [(i, i + by) for i in range(NCTX) if 0 <= i + by < NCTX])


def swap(x):
    return lax.ppermute(x, "ctx", [(i, i ^ 1) for i in range(NCTX)])


def at(y, z, c):
    return (y * 8 + z) * 2 + c


def deliver(x, pairs):
    return lax.ppermute(x, "ctx", pairs)


def exchange(x, pairs):
    to = {i: i ^ 1 for i in range(NCTX)}
    for a, b in pairs:
        to[a], to[b] = b, a
    return lax.ppermute(x, "ctx", sorted(to.items()))


Z_ORDER = (1, 7, 2, 6, 3, 5, 4)
Y_ORDER = (1, 3, 2)
SPREAD = (
    ([(at(0, 0, 0), at(0, 4, 0))],),
    tuple([(at(0, 0, 0), at(0, a, 0)), (at(0, 4, 0), at(0, b, 0))] for a, b in FAN),
    tuple([(at(0, n, 0), at(k, n, 0)) for n in range(8)] for k in Y_ORDER),
)


def spread(held, own, steps):
    for step in steps:
        got = [deliver(held, pairs) for pairs in step]
        for pairs, g in zip(step, got):
            takes = sum([own == b for _, b in pairs], jnp.int32(0)) > 0
            held = jnp.where(takes, g, held)
    return held


def gather_cores(pk, pv, c):
    other = swap(jnp.where(c == 0, pv, pk))
    return jnp.where(c == 0, pk, pv).astype(F32) + other.astype(F32)


def gather_z(part):
    route = exchange if Z_FILL else deliver
    return [
        route(part, [(at(m, n, i), at(m, 0, i)) for m in range(4) for i in range(2)]) for n in Z_ORDER
    ]


def gather_y(part):
    route = exchange if Y_FILL else deliver
    return [route(part, [(at(m, 0, i), at(0, 0, i)) for i in range(2)]) for m in Y_ORDER]


def total_of(part, got):
    return sum([g.astype(F32) for g in got], part)


def on_device(q, k, v, do, doc_lengths):
    own = lax.axis_index("ctx")
    c = own % 2
    core0 = c == 0
    ends = jnp.cumsum(doc_lengths).astype(jnp.int32)
    blocks = own + jnp.arange(8, dtype=jnp.int32)
    pos = blocks[:, None] * TOK + jnp.arange(TOK, dtype=jnp.int32)[None, :]
    starts = jnp.max(jnp.where(ends[:, None, None] <= pos[None], ends[:, None, None], 0), axis=0)
    lo = jnp.where(blocks[:, None] < NCTX, jnp.maximum(starts, PROMPT), FAR)

    info = jnp.concatenate([jnp.stack([own, c]).astype(jnp.int32), lo[:4, 0]])
    place = jnp.stack([own, c]).astype(jnp.int32)

    tok, rows8, prompt, pair = (TOK, WIDE), (8, TOK), (PROMPT, WIDE), (2 * TOK, WIDE)
    turned = (WIDE, TOK)
    smem = pl.BlockSpec(memory_space=pltpu.SMEM)
    vmem = pl.BlockSpec(memory_space=pltpu.VMEM)
    anywhere = pl.BlockSpec(memory_space=pl.ANY)
    kv, qd, sel, held = pl.pallas_call(
        pack_kernel,
        out_shape=[jax.ShapeDtypeStruct(s, BF16) for s in (pair, pair, pair, (2 * PROMPT, WIDE))],
        in_specs=[smem] + [anywhere] * 4,
        out_specs=[vmem] * 4,
        scratch_shapes=[pltpu.SemaphoreType.DMA((4,))],
    )(place, k, v, q, do)

    kv2, qd2 = slide(kv, 2, KV_WRAP), slide(qd, -2, QD_WRAP)
    first = swap(sel)
    stat, acc, do_t = call(
        own_kernel, [(rows8, F32), (turned, F32), (turned, F32)], 1, 140_000_000, info, lo, q, k, v, do
    )
    if SPREAD_GATE:
        held, first = lax.optimization_barrier((held, first))
    held = spread(held, own, SPREAD[:2])
    second = jnp.where(core0, qd2, kv2)
    kv2, qd2, first, second, held, stat, acc, do_t = lax.optimization_barrier(
        (kv2, qd2, first, second, held, stat, acc, do_t)
    )

    second, kv3, qd3 = swap(second), slide(kv2, 1, KV_WRAP), slide(qd2, -1, QD_WRAP)
    if GATE_Y2:
        held, second = lax.optimization_barrier((held, second))
    held = spread(held, own, SPREAD[2:])
    kvp = jnp.where(core0, held, swap(held))
    stat, acc = call(
        near_kernel, [(rows8, F32), (turned, F32)], 1, 280_000_000,
        info, lo, stat, acc, q, second, first, kv2,
    )
    if HALO_DONE:
        kv3, qd3, stat, acc = lax.optimization_barrier((kv3, qd3, stat, acc))
    out_t, rows, pk, pv = call(
        last_kernel, [(turned, F32), (rows8, F32), (prompt, BF16), (prompt, BF16)], 1, 300_000_000,
        info, lo, stat, acc, q, do, do_t, kv3, kvp,
    )

    part = gather_cores(pk, pv, c)
    rows_sent = rows
    if R_AT == "part":
        part, rows_sent = lax.optimization_barrier((part, rows_sent))
    got = gather_z(part.astype(BF16))
    if R_AT == "got":
        got[6], rows_sent = lax.optimization_barrier((got[6], rows_sent))
    att, dq, dk, dv = call(
        query_grad_kernel, [(tok, F32)] * 4, 1, 1_000_000_000,
        info, lo, rows, out_t, q, do, k, v, second, first, kv2, kv3, kvp,
        scratch=[pltpu.VMEM(turned, F32)],
    )
    if R_AT == "dq":
        rows_sent = lax.optimization_barrier((rows, dq))[0]
    if GATE_Z:
        got[0], att, dq, dk, dv = lax.optimization_barrier((got[0], att, dq, dk, dv))
    part = total_of(part, got)
    sent = part.astype(BF16)
    if R_AT == "sent":
        sent, rows_sent = lax.optimization_barrier((sent, rows_sent))
    r1, r2, r3 = shift(rows_sent, -1), shift(rows_sent, -2), shift(rows_sent, -3)
    if DK_WINDOW:
        r1 = lax.optimization_barrier((r1, sent))[0]
    got = gather_y(sent)
    if not DK_WINDOW:
        part = total_of(part, got)
        if GATE_DK:
            r1 = lax.optimization_barrier((r1, part))[0]
    dk, dv, dk_top, dv_top = call(
        key_grad_kernel, [(tok, F32), (tok, F32), (prompt, F32), (prompt, F32)], 1, 900_000_000,
        info, lo, r1, r2, r3, dk, dv, k, v, first, second, qd2, qd3,
        scratch=[pltpu.VMEM(tok, F32), pltpu.VMEM(tok, F32)],
    )
    if DK_WINDOW:
        got[0], dk, dv = lax.optimization_barrier((got[0], dk, dv))
        part = total_of(part, got)
    other = swap(part.astype(BF16))
    dk, dv = pl.pallas_call(
        finish_kernel,
        out_shape=[jax.ShapeDtypeStruct(tok, F32)] * 2,
        in_specs=[smem] + [vmem] * 4 + [anywhere] * 2,
        out_specs=[anywhere] * 2,
        scratch_shapes=[pltpu.VMEM(prompt, F32), pltpu.VMEM(prompt, F32), pltpu.SemaphoreType.DMA((2,))],
        input_output_aliases={5: 0, 6: 1},
        compiler_params=pltpu.CompilerParams(vmem_limit_bytes=VMEM_LIMIT),
    )(info, part, other, dk_top, dv_top, dk, dv)
    return att, dq, dk, dv


def solution(mesh):
    spec = P("ctx", "head")
    return jax.shard_map(
        on_device, mesh=mesh, in_specs=(spec,) * 4 + (P(),), out_specs=(spec,) * 4, check_vma=False
    )
```
